512 devices in a mesh: row: 8 (over z), col: 16 (over y, core), layer: 4 (over x).
Axes of the slice: x: 4, y: 8, z: 8, core: 2. Of those that a mesh axis runs over, the one named last changes fastest.
Arguments:
- panel_values: bfloat16 [16384, 8192], P('row', ('layer', 'col')), may hold values from -6 to 6
- slab_values: bfloat16 [8192, 6144], P(('layer', 'row'), 'col'), may hold values from -0.09375 to 0.09375
- pattern_panel: int32 [128, 64], P('row', ('layer', 'col')), may hold values from 0 to 1, as said below
- pattern_result: int32 [128, 48], P(('row', 'layer'), 'col'), may hold values 0 or 1
Outputs:
- product_slab: bfloat16 [16384, 6144], P(('row', 'layer'), 'col')
The draws below stay inside these ranges and needn't reach their ends.
Inputs may be any that keep to these rules, and one draw needn't show every extreme that they name: `pattern_panel`: in every group of 16 blocks that one device holds of one block column (block rows r * 16 to r * 16 + 15), 1 to 8 are 1; some group reaches this bound: every group of block column 0 has exactly 8.
All inputs are finite; a program needn't handle non-finite values. No bound on the sum of `pattern_result` on one device may be relied on, other than what follows from the above.
Results may differ from the reference program's by a relative error of at most 0.001.
Values may be sent and summed in bfloat16 or wider, within the bound.
A program may use at most 64 MiB of HBM per device.

```python
import jax
import jax.numpy as jnp
from jax import lax

BS = 128
RB_DEV = 16
NNZ = 8
NR = 128
NK = 64
NC = 48
N_ROW = 8


def draw_pattern_panel(key, part):
    key = jax.random.fold_in(key, 11)
    key_order, key_count = jax.random.split(key)
    shape_full = (N_ROW, RB_DEV, NK)
    scores = jax.random.randint(key_order, shape_full, 0, 1 << 20) * RB_DEV + lax.broadcasted_iota(jnp.int32, shape_full, 1)
    ranking = jnp.argsort(jnp.argsort(scores, axis=1), axis=1).astype(jnp.int32)
    counts = jax.random.randint(key_count, (N_ROW, 1, NK), 1, NNZ + 1)
    counts = counts.at[:, :, 0].set(NNZ)
    return (ranking < counts).astype(jnp.int32).reshape(N_ROW * RB_DEV, NK)


def plant(array, own_key, low, top_value):
    spot = [jax.random.randint(jax.random.fold_in(own_key, axis), (), 0, length) for axis, length in enumerate(array.shape)]
    main_axis = array.shape.index(max(array.shape))
    beside = spot[:main_axis] + [(spot[main_axis] + 1) % array.shape[main_axis]] + spot[main_axis + 1:]
    return array.at[tuple(spot)].set(low).at[tuple(beside)].set(top_value)


def level_of(stream_key, dims, shards, low, largest):
    factor_of = 1.0
    for dim, shards_of in shards:
        draws = jax.random.uniform(jax.random.fold_in(jax.random.fold_in(stream_key, 6), dim), (shards_of,), jnp.float32, low / len(shards), largest / len(shards))
        factor_of = factor_of * jnp.repeat(jnp.exp(draws), dims[dim] // shards_of).reshape((-1,) + (1,) * (len(dims) - 1 - dim))
    return factor_of


def gaussian(stream_key, shape, deviation, reach, cuts=(), kind=jnp.bfloat16):
    values = jax.random.normal(stream_key, shape, jnp.float32) * deviation
    if len(cuts) > 0:
        values = level_of(stream_key, shape, cuts, -0.22, 0.18) * values
    return jnp.clip(values, min=-reach, max=reach).astype(kind)


def setup_inputs(seed: int = 0) -> dict:
    arg_keys = jax.random.split(jax.random.key(seed), 5)
    panel_values = gaussian(arg_keys[0], (NR * BS, NK * BS), 1.0, 6.0, ((0, 8), (1, 64)))
    slab_values = gaussian(arg_keys[1], (NK * BS, NC * BS), (NK * BS // 2) ** -0.5, 0.09375, ((0, 32), (1, 16)))
    pattern_panel = draw_pattern_panel(jax.random.fold_in(arg_keys[4], 71), 0)
    pattern_result = plant((jax.random.randint(arg_keys[3], (NR, NC), 0, 4) < 3).astype(jnp.int32), jax.random.fold_in(arg_keys[3], 1), 0, 1)
    return dict(panel_values=panel_values, slab_values=slab_values, pattern_panel=pattern_panel, pattern_result=pattern_result)


def reference(panel_values, slab_values, pattern_panel, pattern_result):
    rows_total = panel_values.shape[0] // BS
    inner_total = panel_values.shape[1] // BS
    cols_total = slab_values.shape[1] // BS
    weights = pattern_panel.astype(jnp.bfloat16)
    masked = panel_values.reshape(rows_total, BS, inner_total, BS) * weights[:, None, :, None]
    masked = masked.reshape(panel_values.shape)
    product = jnp.dot(masked, slab_values, preferred_element_type=jnp.float32)
    keeper = pattern_result.astype(jnp.float32)
    filtered = product.reshape(rows_total, BS, cols_total, BS) * keeper[:, None, :, None]
    return filtered.reshape(product.shape).astype(jnp.bfloat16)
```

```python
import functools

import jax
import jax.numpy as jnp
from jax import lax
from jax.experimental import pallas as pl
from jax.experimental.pallas import tpu as pltpu
from jax.sharding import PartitionSpec as P

BS = 128
RB = 16
NNZ = 8
TAB = 16
NL = 4
UNITS = ((2, 0), (2, 1), (1, 1), (3, 0), (1, 0), (3, 1), (0, 0), (0, 1))
Y_STEP, Z_STEP = 1.31, 1.97


def ring_order(n, pieces, forward):
    order = []
    own = pieces if forward else pieces[::-1]
    for step in range(n // 2):
        order += [(step, q) for q in (own if step < n // 2 - 1 else own[:1])]
    return order


def kernel(n, panel_hbm, slab_hbm, flags, keep, out, *scratch):
    held = scratch[: 2 * n]
    (panel, slab, dense, send_x, mid_x, last_x, own_sem, y_send, y_recv, c_send, c_recv, z_send, z_recv, x_send, x_recv) = scratch[2 * n :]
    col, z, layer = lax.axis_index("col"), lax.axis_index("row"), lax.axis_index("layer")
    y, core = col // 2, lax.rem(col, 2)
    depth = slab_hbm.shape[0]
    part = depth // 2

    panel_in = pltpu.make_async_copy(panel_hbm, panel, own_sem.at[0])
    panel_in.start()
    slab_in = pltpu.make_async_copy(slab_hbm, slab.at[pl.ds(pl.multiple_of(z * depth, depth), depth)], own_sem.at[1])
    slab_in.start()

    def beside(place, count, step):
        return lax.rem(place + step + count, count)

    y_next = {+1: {"col": beside(y, n, 1) * 2 + core}, -1: {"col": beside(y, n, -1) * 2 + core}}
    z_next = {+1: {"row": beside(z, n, 1)}, -1: {"row": beside(z, n, -1)}}
    x_next = {+1: {"layer": beside(layer, NL, 1)}, -1: {"layer": beside(layer, NL, -1)}}
    sibling = {"col": y * 2 + 1 - core}
    neighbours = [y_next[1], y_next[-1], z_next[1], z_next[-1], x_next[1], x_next[-1], sibling]
    barrier = pltpu.get_barrier_semaphore()
    for device in neighbours:
        pl.semaphore_signal(barrier, inc=1, device_id=device, device_id_type=pl.DeviceIdType.MESH)

    rows_of = []
    for ahead, half in UNITS:
        first = lax.rem(layer + ahead, NL) * (RB // NL) + half * 2
        rows_of += [first, first + 1]
    count = jnp.int32(0)
    source = [jnp.int32(0)] * NNZ
    table = jnp.full((TAB, BS), float(NNZ), jnp.float32)
    place_of = lax.broadcasted_iota(jnp.int32, (TAB, BS), 0)
    for p in range(RB):
        flag = flags[rows_of[p]]
        if p > RB - NNZ:
            count = jnp.maximum(count, p - (RB - NNZ))
        for s in range(max(0, p - (RB - NNZ)), min(p, NNZ - 1) + 1):
            source[s] = jnp.where((flag == 1) & (count == s), rows_of[p], source[s])
        slot = jnp.where(flag == 1, count, NNZ)
        table = jnp.where(place_of == p, slot.astype(jnp.float32), table)
        count = count + flag
    held[0][pl.ds(0, TAB), :] = table.astype(jnp.bfloat16)
    panel_in.wait()
    for s in range(NNZ):
        held[0][pl.ds(TAB + s * BS, BS), :] = panel[source[s]]
    slab_in.wait()
    pl.semaphore_wait(barrier, len(neighbours))

    started = []

    def remote(src, dst, send, recv, device):
        return pltpu.make_async_remote_copy(src_ref=src, dst_ref=dst, send_sem=send, recv_sem=recv, device_id=device, device_id_type=pl.DeviceIdType.MESH)

    def begin(copy):
        copy.start()
        started.append(copy)

    def rows(q):
        return pl.ds(0, TAB + 2 * BS) if q == 0 else pl.ds(TAB + q * 2 * BS, 2 * BS)

    y_order = {d: ring_order(n, [0, 1], d == 1) + ring_order(n, [2, 3], d == 1) for d in (1, -1)}
    z_order = {d: ring_order(n, [0, 1], d == 1) for d in (1, -1)}

    def y_copy(d, i):
        step, q = y_order[d][i]
        src, dst = held[2 * ((-d * step) % n)], held[2 * ((-d * (step + 1)) % n)]
        k = (0 if d == 1 else len(y_order[1])) + i
        return remote(src.at[rows(q)], dst.at[rows(q)], y_send.at[k], y_recv.at[k], y_next[d])

    def c_copy(j, q):
        return remote(held[2 * j].at[rows(q)], held[2 * j + 1].at[rows(q)], c_send.at[4 * j + q], c_recv.at[4 * j + q], sibling)

    def z_copy(d, i, back=0):
        step, q = z_order[d][i]
        k = (0 if d == 1 else len(z_order[1])) + i
        at = slab.at[pl.ds(pl.multiple_of(beside(z, n, -d * (step + back)) * depth + q * part, part), part)]
        return remote(at, at, z_send.at[k], z_recv.at[k], z_next[d])

    def lanes(j, c):
        side = core if c == 0 else 1 - core
        return pl.ds(pl.multiple_of(beside(y, n, j) * 2 * BS + side * BS, BS), BS)

    def unpack(j, c, places):
        ref, where = held[2 * j + c], lanes(j, c)
        slots = range(min(NNZ, places[-1] + 1))
        one_of = {}
        for p in places:
            line = ref[pl.ds(0, TAB), :][p : p + 1, :].astype(jnp.float32)
            for s in slots:
                if p - (RB - NNZ) <= s <= p:
                    one_of[p, s] = (line == float(s)).astype(jnp.bfloat16)

        @pl.loop(0, BS // 16)
        def _(i):
            values = [ref[pl.ds(pl.multiple_of(TAB + s * BS + i * 16, 16), 16), :] for s in slots]
            for p in places:
                terms = [values[s] * one_of[p, s] for s in slots if (p, s) in one_of]
                dense[pl.ds(pl.multiple_of(p * BS + i * 16, 16), 16), where] = functools.reduce(jnp.add, terms)

    def multiply(unit):
        return jnp.dot(dense[pl.ds(unit * 2 * BS, 2 * BS), :], slab[...], preferred_element_type=jnp.float32)

    def x_copy(k, device, dst):
        return remote(send_x.at[k], dst, x_send.at[k], x_recv.at[k], device)

    x_copies = [
        x_copy(0, x_next[1], mid_x.at[0]),
        x_copy(1, x_next[-1], mid_x.at[1]),
        x_copy(2, x_next[1], last_x.at[0]),
        x_copy(3, x_next[-1], last_x.at[1]),
        x_copy(4, x_next[1], last_x.at[2]),
        x_copy(5, x_next[-1], last_x.at[3]),
    ]

    for d in (1, -1):
        for i in range(min(2, len(y_order[d]))):
            if y_order[d][i][0] == 0:
                begin(y_copy(d, i))
        for i in range(min(2, len(z_order[d]))):
            begin(z_copy(d, i))
    for q in range(4):
        begin(c_copy(0, q))

    arrived, passed = {0: {0, 1, 2, 3}}, {0: {0, 1, 2, 3}}
    early, late = list(range(RB // NL)), list(range(RB // NL, RB))
    done = set()
    waited = set()

    def take(j, c, wanted, which):
        if (j, c, which) in done:
            return
        if c == 1:
            for q in wanted:
                if (j, q) not in waited:
                    waited.add((j, q))
                    c_copy(j, q).wait_recv()
        done.add((j, c, which))
        unpack(j, c, early if which == 0 else late)

    def drain(c, source_of):
        for j in range(n):
            have = source_of.get(j, set())
            if {0, 1} <= have:
                take(j, c, (0, 1), 0)
            if {0, 1, 2, 3} <= have:
                take(j, c, (0, 1, 2, 3), 1)

    events = [(Y_STEP * (i + 1), 0, i) for i in range(len(y_order[1]))] + [(Z_STEP * (i + 1), 1, i) for i in range(len(z_order[1]))]
    computed = [0]

    def early_unit(u):
        send_x[u] = multiply(u)
        begin(x_copies[u])

    z_left = len(z_order[1])
    for _, kind, i in sorted(events):
        if kind == 1:
            for d in (1, -1):
                z_copy(d, i, 1).wait_recv()
                if i + 2 < len(z_order[d]):
                    begin(z_copy(d, i + 2))
            z_left -= 1
            continue
        before = {j: set(v) for j, v in passed.items()}
        for d in (1, -1):
            step, q = y_order[d][i]
            j = (-d * (step + 1)) % n
            y_copy(d, i).wait_recv()
            if i + 2 < len(y_order[d]):
                begin(y_copy(d, i + 2))
            begin(c_copy(j, q))
            arrived.setdefault(j, set()).add(q)
            passed.setdefault(j, set()).add(q)
        if i < len(y_order[1]) - 1:
            drain(0, arrived)
            drain(1, before)
            ready = all((j, c, 0) in done for j in range(n) for c in range(2))
            if z_left == 0 and ready and computed[0] < 2:
                early_unit(computed[0])
                computed[0] += 1
    drain(0, arrived)
    drain(1, passed)
    for u in range(computed[0], 2):
        early_unit(u)
    for u in (2, 3):
        early_unit(u)
    for u, k in ((4, 0), (5, 1)):
        own = multiply(u)
        x_copies[k].wait_recv()
        send_x[u] = own + mid_x[k]
        begin(x_copies[u])
    top, low = multiply(6), multiply(7)
    half = 2 * BS

    def finish(total, first):
        for r in range(2):
            for c in range(total.shape[1] // BS):
                kept = keep[first // BS + r, c].astype(jnp.float32)
                out[pl.ds(first + r * BS, BS), pl.ds(c * BS, BS)] = (total[r * BS : (r + 1) * BS, c * BS : (c + 1) * BS] * kept).astype(jnp.bfloat16)

    x_copies[3].wait_recv()
    send_top = top + last_x[1]
    x_copies[2].wait_recv()
    send_low = low + last_x[0]
    x_copies[4].wait_recv()
    finish(send_top + last_x[2], 0)
    x_copies[5].wait_recv()
    finish(send_low + last_x[3], half)
    for copy in started:
        copy.wait_send()


def per_device(n, panel_values, slab_values, pattern_panel, pattern_result):
    block = panel_values.shape[1]
    width = slab_values.shape[1]
    depth = slab_values.shape[0]
    sent_y, sent_z = len(ring_order(n, [0, 1], True)) * 2, len(ring_order(n, [0, 1], True))
    dma = pltpu.SemaphoreType.DMA
    held = [pltpu.VMEM((TAB + NNZ * BS, BS), jnp.bfloat16) for _ in range(2 * n)]
    half = 2 * BS
    return pl.pallas_call(
        functools.partial(kernel, n),
        out_shape=jax.ShapeDtypeStruct((4 * BS, width), jnp.bfloat16),
        in_specs=[
            pl.BlockSpec(memory_space=pl.ANY),
            pl.BlockSpec(memory_space=pl.ANY),
            pl.BlockSpec(memory_space=pltpu.SMEM),
            pl.BlockSpec(memory_space=pltpu.SMEM),
        ],
        out_specs=pl.BlockSpec(memory_space=pltpu.VMEM),
        scratch_shapes=held
        + [
            pltpu.VMEM((RB, BS, BS), jnp.bfloat16),
            pltpu.VMEM((n * depth, width), jnp.bfloat16),
            pltpu.VMEM((RB * BS, n * 2 * BS), jnp.bfloat16),
            pltpu.VMEM((6, half, width), jnp.float32),
            pltpu.VMEM((2, half, width), jnp.float32),
            pltpu.VMEM((4, half, width), jnp.float32),
            dma((2,)),
            dma((2 * sent_y,)),
            dma((2 * sent_y,)),
            dma((4 * n,)),
            dma((4 * n,)),
            dma((2 * sent_z,)),
            dma((2 * sent_z,)),
            dma((6,)),
            dma((6,)),
        ],
        compiler_params=pltpu.CompilerParams(collective_id=0, has_side_effects=True, vmem_limit_bytes=48 * 1024 * 1024),
        cost_estimate=pl.CostEstimate(flops=2 * RB * BS * n * 2 * BS * width, bytes_accessed=1 << 22, transcendentals=0),
    )(panel_values.reshape(RB, BS, block), slab_values, pattern_panel[:, 0], pattern_result)


def solution(mesh):
    placed = (
        P("row", ("layer", "col")),
        P(("layer", "row"), "col"),
        P("row", ("layer", "col")),
        P(("row", "layer"), "col"),
    )
    return jax.shard_map(
        functools.partial(per_device, mesh.shape["row"]),
        mesh=mesh,
        in_specs=placed,
        out_specs=P(("row", "layer"), "col"),
        check_vma=False,
    )
```

```python
import functools

import jax
import jax.numpy as jnp
from jax import lax
from jax.experimental import pallas as pl
from jax.experimental.pallas import tpu as pltpu
from jax.sharding import PartitionSpec as P

BS = 128
RB = 16
NNZ = 8
TAB = 16
NL = 4
UNITS = ((2, 0), (2, 1), (1, 1), (3, 0), (1, 0), (3, 1), (0, 0), (0, 1))
Y_STEP, Z_STEP = 1.7, 2.45


def ring_order(n, forward, pieces):
    own = list(range(pieces)) if forward else list(range(pieces))[::-1]
    return [(step, q) for step in range(n // 2) for q in (own if step < n // 2 - 1 else own[: pieces // 2])]


def panel_order(n, forward):
    a, b, c, d = (0, 1, 2, 3) if forward else (1, 0, 3, 2)
    last = n // 2 - 1
    place = {}
    for step in range(n // 2):
        for q, at in ((a, 3 * step), (b, 3 * step + 1), (c, 3 * step + 2 + 3 * (step > 0)), (d, 3 * step + 5.5 + (step > 0) * 1.5)):
            if step < last or q in (a, c):
                place[step, q] = at
    return sorted(place, key=place.get)


def triggers(order, depth):
    after = []
    for m, (step, q) in enumerate(order):
        needs = order.index((step - 1, q)) if step else -1
        after.append(max(after[-1] if after else -1, needs, m - depth))
    return after


def kernel(n, panel_hbm, slab_hbm, flags_hbm, keep_hbm, out, *scratch):
    held = scratch[: 2 * n]
    (flags, keep, panel, slab, dense, send_x, mid_x, last_x, own_sem, y_send, y_recv, c_send, c_recv, z_send, z_recv, x_send, x_recv) = scratch[2 * n :]
    col, z, layer = lax.axis_index("col"), lax.axis_index("row"), lax.axis_index("layer")
    y, core = col // 2, lax.rem(col, 2)
    depth = slab_hbm.shape[0]
    part = depth // 2

    def beside(place, count, step):
        return lax.rem(place + step + count, count)

    y_next = {+1: {"col": beside(y, n, 1) * 2 + core}, -1: {"col": beside(y, n, -1) * 2 + core}}
    z_next = {+1: {"row": beside(z, n, 1)}, -1: {"row": beside(z, n, -1)}}
    x_next = {+1: {"layer": beside(layer, NL, 1)}, -1: {"layer": beside(layer, NL, -1)}}
    sibling = {"col": y * 2 + 1 - core}
    neighbours = [y_next[1], y_next[-1], z_next[1], z_next[-1], x_next[1], x_next[-1], sibling]
    barrier = pltpu.get_barrier_semaphore()
    for device in neighbours:
        pl.semaphore_signal(barrier, inc=1, device_id=device, device_id_type=pl.DeviceIdType.MESH)

    flags_in = pltpu.make_async_copy(flags_hbm, flags, own_sem.at[0])
    flags_in.start()
    panel_in = pltpu.make_async_copy(panel_hbm, panel, own_sem.at[1])
    panel_in.start()
    slab_in = pltpu.make_async_copy(slab_hbm, slab.at[pl.ds(pl.multiple_of(z * depth, depth), depth)], own_sem.at[2])
    slab_in.start()
    keep_in = pltpu.make_async_copy(keep_hbm, keep, own_sem.at[3])
    keep_in.start()

    rows_of = []
    for ahead, half in UNITS:
        first = lax.rem(layer + ahead, NL) * (RB // NL) + half * 2
        rows_of += [first, first + 1]
    count = jnp.int32(0)
    source = [jnp.int32(0)] * NNZ
    table = jnp.full((TAB, BS), float(NNZ), jnp.float32)
    place_of = lax.broadcasted_iota(jnp.int32, (TAB, BS), 0)
    flags_in.wait()
    for p in range(RB):
        flag = flags[rows_of[p]]
        if p > RB - NNZ:
            count = jnp.maximum(count, p - (RB - NNZ))
        for s in range(max(0, p - (RB - NNZ)), min(p, NNZ - 1) + 1):
            source[s] = jnp.where((flag == 1) & (count == s), rows_of[p], source[s])
        slot = jnp.where(flag == 1, count, NNZ)
        table = jnp.where(place_of == p, slot.astype(jnp.float32), table)
        count = count + flag
    held[0][pl.ds(0, TAB), :] = table.astype(jnp.bfloat16)
    panel_in.wait()

    def pack(q):
        for s in (2 * q, 2 * q + 1):
            held[0][pl.ds(TAB + s * BS, BS), :] = panel[source[s]]

    pack(0)
    pack(1)
    slab_in.wait()
    keep_in.wait()
    pl.semaphore_wait(barrier, len(neighbours))

    started = []

    def remote(src, dst, send, recv, device):
        return pltpu.make_async_remote_copy(src_ref=src, dst_ref=dst, send_sem=send, recv_sem=recv, device_id=device, device_id_type=pl.DeviceIdType.MESH)

    def begin(copy):
        copy.start()
        started.append(copy)

    def rows(q):
        return pl.ds(0, TAB + 2 * BS) if q == 0 else pl.ds(TAB + q * 2 * BS, 2 * BS)

    y_order = {d: panel_order(n, d == 1) for d in (1, -1)}
    z_order = {d: ring_order(n, d == 1, 2) for d in (1, -1)}
    y_after, z_after = triggers(y_order[1], 4), triggers(z_order[1], 2)

    def y_copy(d, i):
        step, q = y_order[d][i]
        src, dst = held[2 * ((-d * step) % n)], held[2 * ((-d * (step + 1)) % n)]
        k = (0 if d == 1 else len(y_order[1])) + i
        return remote(src.at[rows(q)], dst.at[rows(q)], y_send.at[k], y_recv.at[k], y_next[d])

    def c_copy(j, q):
        return remote(held[2 * j].at[rows(q)], held[2 * j + 1].at[rows(q)], c_send.at[4 * j + q], c_recv.at[4 * j + q], sibling)

    def z_copy(d, i, back=0):
        step, q = z_order[d][i]
        k = (0 if d == 1 else len(z_order[1])) + i
        at = slab.at[pl.ds(pl.multiple_of(beside(z, n, -d * (step + back)) * depth + q * part, part), part)]
        return remote(at, at, z_send.at[k], z_recv.at[k], z_next[d])

    def lanes(j, c):
        side = core if c == 0 else 1 - core
        return pl.ds(pl.multiple_of(beside(y, n, j) * 2 * BS + side * BS, BS), BS)

    def unpack(j, c, places):
        ref, where = held[2 * j + c], lanes(j, c)
        slots = range(min(NNZ, places[-1] + 1))
        one_of = {}
        for p in places:
            line = ref[pl.ds(0, TAB), :][p : p + 1, :].astype(jnp.float32)
            for s in slots:
                if p - (RB - NNZ) <= s <= p:
                    one_of[p, s] = (line == float(s)).astype(jnp.bfloat16)

        @pl.loop(0, BS // 16)
        def _(i):
            values = [ref[pl.ds(pl.multiple_of(TAB + s * BS + i * 16, 16), 16), :] for s in slots]
            for p in places:
                terms = [values[s] * one_of[p, s] for s in slots if (p, s) in one_of]
                dense[pl.ds(pl.multiple_of(p * BS + i * 16, 16), 16), where] = functools.reduce(jnp.add, terms)

    def multiply(unit):
        return jnp.dot(dense[pl.ds(unit * 2 * BS, 2 * BS), :], slab[...], preferred_element_type=jnp.float32)

    def x_copy(k, device, dst):
        return remote(send_x.at[k], dst, x_send.at[k], x_recv.at[k], device)

    x_copies = [
        x_copy(0, x_next[1], mid_x.at[0]),
        x_copy(1, x_next[-1], mid_x.at[1]),
        x_copy(2, x_next[1], last_x.at[0]),
        x_copy(3, x_next[-1], last_x.at[1]),
        x_copy(4, x_next[1], last_x.at[2]),
        x_copy(5, x_next[-1], last_x.at[3]),
    ]

    def follow(copy_of, after, event):
        for i, at in enumerate(after):
            if at == event:
                for d in (1, -1):
                    begin(copy_of(d, i))

    first, rest = [(d, i) for i, at in enumerate(y_after) if at == -1 for d in (1, -1)], (2, 3)
    for d, i in first[:4] if n > 2 else ():
        begin(y_copy(d, i))
    follow(z_copy, z_after, -1)
    for q in rest:
        pack(q)
    for d, i in first[4:] if n > 2 else first:
        begin(y_copy(d, i))
    for q in range(4):
        begin(c_copy(0, q))

    arrived, passed = {0: {0, 1, 2, 3}}, {0: {0, 1, 2, 3}}
    early, late = list(range(RB // NL)), list(range(RB // NL, RB))
    done = set()
    waited = set()

    def take(j, c, wanted, which):
        if (j, c, which) in done:
            return
        if c == 1:
            for q in wanted:
                if (j, q) not in waited:
                    waited.add((j, q))
                    c_copy(j, q).wait_recv()
        done.add((j, c, which))
        unpack(j, c, early if which == 0 else late)

    def drain(c, source_of):
        for j in range(n):
            have = source_of.get(j, set())
            if {0, 1} <= have:
                take(j, c, (0, 1), 0)
            if {0, 1, 2, 3} <= have:
                take(j, c, (0, 1, 2, 3), 1)

    events = [(Y_STEP * (i + 1), 0, i) for i in range(len(y_order[1]))] + [(Z_STEP * (i + 1), 1, i) for i in range(len(z_order[1]))]
    computed = [0]

    def early_unit(u):
        send_x[u] = multiply(u)
        begin(x_copies[u])

    z_left = len(z_order[1])
    for _, kind, i in sorted(events):
        if kind == 1:
            for d in (1, -1):
                z_copy(d, i, 1).wait_recv()
            follow(z_copy, z_after, i)
            z_left -= 1
            continue
        before = {j: set(v) for j, v in passed.items()}
        for d in (1, -1):
            step, q = y_order[d][i]
            j = (-d * (step + 1)) % n
            y_copy(d, i).wait_recv()
            begin(c_copy(j, q))
            arrived.setdefault(j, set()).add(q)
            passed.setdefault(j, set()).add(q)
        follow(y_copy, y_after, i)
        if i < len(y_order[1]) - 1:
            drain(0, arrived)
            drain(1, before)
            ready = all((j, c, 0) in done for j in range(n) for c in range(2))
            if z_left == 0 and ready and computed[0] < 2:
                early_unit(computed[0])
                computed[0] += 1
    drain(0, arrived)
    drain(1, passed)
    for u in range(computed[0], 2):
        early_unit(u)
    for u in (2, 3):
        early_unit(u)
    for u, k in ((4, 0), (5, 1)):
        own = multiply(u)
        x_copies[k].wait_recv()
        send_x[u] = own + mid_x[k]
        begin(x_copies[u])
    top, low = multiply(6), multiply(7)
    half = 2 * BS

    def finish(total, first):
        for r in range(2):
            for c in range(total.shape[1] // BS):
                kept = keep[first // BS + r, c].astype(jnp.float32)
                out[pl.ds(first + r * BS, BS), pl.ds(c * BS, BS)] = (total[r * BS : (r + 1) * BS, c * BS : (c + 1) * BS] * kept).astype(jnp.bfloat16)

    x_copies[3].wait_recv()
    send_top = top + last_x[1]
    x_copies[2].wait_recv()
    send_low = low + last_x[0]
    x_copies[4].wait_recv()
    finish(send_top + last_x[2], 0)
    x_copies[5].wait_recv()
    finish(send_low + last_x[3], half)
    for copy in started:
        copy.wait_send()


def per_device(n, panel_values, slab_values, pattern_panel, pattern_result):
    block = panel_values.shape[1]
    width = slab_values.shape[1]
    depth = slab_values.shape[0]
    sent_y, sent_z = len(panel_order(n, True)), len(ring_order(n, True, 2))
    dma = pltpu.SemaphoreType.DMA
    held = [pltpu.VMEM((TAB + NNZ * BS, BS), jnp.bfloat16) for _ in range(2 * n)]
    half = 2 * BS
    return pl.pallas_call(
        functools.partial(kernel, n),
        out_shape=jax.ShapeDtypeStruct((4 * BS, width), jnp.bfloat16),
        in_specs=[pl.BlockSpec(memory_space=pl.ANY)] * 4,
        out_specs=pl.BlockSpec(memory_space=pltpu.VMEM),
        scratch_shapes=held
        + [
            pltpu.SMEM((RB,), jnp.int32),
            pltpu.SMEM(pattern_result.shape, jnp.int32),
            pltpu.VMEM((RB, BS, BS), jnp.bfloat16),
            pltpu.VMEM((n * depth, width), jnp.bfloat16),
            pltpu.VMEM((RB * BS, n * 2 * BS), jnp.bfloat16),
            pltpu.VMEM((6, half, width), jnp.float32),
            pltpu.VMEM((2, half, width), jnp.float32),
            pltpu.VMEM((4, half, width), jnp.float32),
            dma((4,)),
            dma((2 * sent_y,)),
            dma((2 * sent_y,)),
            dma((4 * n,)),
            dma((4 * n,)),
            dma((2 * sent_z,)),
            dma((2 * sent_z,)),
            dma((6,)),
            dma((6,)),
        ],
        compiler_params=pltpu.CompilerParams(collective_id=0, has_side_effects=True, vmem_limit_bytes=60 * 1024 * 1024),
        cost_estimate=pl.CostEstimate(flops=2 * RB * BS * n * 2 * BS * width, bytes_accessed=1 << 22, transcendentals=0),
    )(panel_values.reshape(RB, BS, block), slab_values, pattern_panel[:, 0], pattern_result)


def solution(mesh):
    placed = (
        P("row", ("layer", "col")),
        P(("layer", "row"), "col"),
        P("row", ("layer", "col")),
        P(("row", "layer"), "col"),
    )
    return jax.shard_map(
        functools.partial(per_device, mesh.shape["row"]),
        mesh=mesh,
        in_specs=placed,
        out_specs=P(("row", "layer"), "col"),
        check_vma=False,
    )
```

```python
import functools

import jax
import jax.numpy as jnp
from jax import lax
from jax.experimental import pallas as pl
from jax.experimental.pallas import tpu as pltpu
from jax.sharding import PartitionSpec as P

BS = 128
RB = 16
NNZ = 8
TAB = 16
NL = 4
UNITS = ((2, 0), (2, 1), (1, 1), (3, 0), (1, 0), (3, 1), (0, 0), (0, 1))
GROUP = 32
TOP = 32767.0
Y_STEP, Z_STEP = 1.7, 2.45


def ring_order(n, forward, pieces):
    own = list(range(pieces)) if forward else list(range(pieces))[::-1]
    return [(step, q) for step in range(n // 2) for q in (own if step < n // 2 - 1 else own[: pieces // 2])]


def panel_order(n, forward):
    a, b, c, d = (0, 1, 2, 3) if forward else (1, 0, 3, 2)
    last = n // 2 - 1
    place = {}
    for step in range(n // 2):
        for q, at in ((a, 3 * step), (b, 3 * step + 1), (c, 3 * step + 2 + 3 * (step > 0)), (d, 3 * step + 5.5 + (step > 0) * 1.5)):
            if step < last or q in (a, c):
                place[step, q] = at
    return sorted(place, key=place.get)


def triggers(order, depth):
    after = []
    for m, (step, q) in enumerate(order):
        needs = order.index((step - 1, q)) if step else -1
        after.append(max(after[-1] if after else -1, needs, m - depth))
    return after


def kernel(n, panel_hbm, slab_hbm, flags_hbm, keep_hbm, out, *scratch):
    held = scratch[: 2 * n]
    (flags, keep, panel, slab, dense, own, send_x, send_s, got_x, got_s, own_sem, y_send, y_recv, c_send, c_recv, z_send, z_recv, x_send, x_recv, s_send, s_recv) = scratch[2 * n :]
    col, z, layer = lax.axis_index("col"), lax.axis_index("row"), lax.axis_index("layer")
    y, core = col // 2, lax.rem(col, 2)
    depth = slab_hbm.shape[0]
    part = depth // 2

    def beside(place, count, step):
        return lax.rem(place + step + count, count)

    y_next = {+1: {"col": beside(y, n, 1) * 2 + core}, -1: {"col": beside(y, n, -1) * 2 + core}}
    z_next = {+1: {"row": beside(z, n, 1)}, -1: {"row": beside(z, n, -1)}}
    x_next = {+1: {"layer": beside(layer, NL, 1)}, -1: {"layer": beside(layer, NL, -1)}}
    sibling = {"col": y * 2 + 1 - core}
    neighbours = [y_next[1], y_next[-1], z_next[1], z_next[-1], x_next[1], x_next[-1], sibling]
    barrier = pltpu.get_barrier_semaphore()
    for device in neighbours:
        pl.semaphore_signal(barrier, inc=1, device_id=device, device_id_type=pl.DeviceIdType.MESH)

    flags_in = pltpu.make_async_copy(flags_hbm, flags, own_sem.at[0])
    flags_in.start()
    panel_in = pltpu.make_async_copy(panel_hbm, panel, own_sem.at[1])
    panel_in.start()
    slab_in = pltpu.make_async_copy(slab_hbm, slab.at[pl.ds(pl.multiple_of(z * depth, depth), depth)], own_sem.at[2])
    slab_in.start()
    keep_in = pltpu.make_async_copy(keep_hbm, keep, own_sem.at[3])
    keep_in.start()

    rows_of = []
    for ahead, half in UNITS:
        first = lax.rem(layer + ahead, NL) * (RB // NL) + half * 2
        rows_of += [first, first + 1]
    count = jnp.int32(0)
    source = [jnp.int32(0)] * NNZ
    table = jnp.full((TAB, BS), float(NNZ), jnp.float32)
    place_of = lax.broadcasted_iota(jnp.int32, (TAB, BS), 0)
    flags_in.wait()
    for p in range(RB):
        flag = flags[rows_of[p]]
        if p > RB - NNZ:
            count = jnp.maximum(count, p - (RB - NNZ))
        for s in range(max(0, p - (RB - NNZ)), min(p, NNZ - 1) + 1):
            source[s] = jnp.where((flag == 1) & (count == s), rows_of[p], source[s])
        slot = jnp.where(flag == 1, count, NNZ)
        table = jnp.where(place_of == p, slot.astype(jnp.float32), table)
        count = count + flag
    held[0][pl.ds(0, TAB), :] = table.astype(jnp.bfloat16)
    panel_in.wait()

    def pack(q):
        for s in (2 * q, 2 * q + 1):
            held[0][pl.ds(TAB + s * BS, BS), :] = panel[source[s]]

    pack(0)
    pack(1)
    slab_in.wait()
    keep_in.wait()
    pl.semaphore_wait(barrier, len(neighbours))

    started = []

    def remote(src, dst, send, recv, device):
        return pltpu.make_async_remote_copy(src_ref=src, dst_ref=dst, send_sem=send, recv_sem=recv, device_id=device, device_id_type=pl.DeviceIdType.MESH)

    def begin(copy):
        copy.start()
        started.append(copy)

    def rows(q):
        return pl.ds(0, TAB + 2 * BS) if q == 0 else pl.ds(TAB + q * 2 * BS, 2 * BS)

    y_order = {d: panel_order(n, d == 1) for d in (1, -1)}
    z_order = {d: ring_order(n, d == 1, 2) for d in (1, -1)}
    y_after, z_after = triggers(y_order[1], 4), triggers(z_order[1], 2)

    def y_copy(d, i):
        step, q = y_order[d][i]
        src, dst = held[2 * ((-d * step) % n)], held[2 * ((-d * (step + 1)) % n)]
        k = (0 if d == 1 else len(y_order[1])) + i
        return remote(src.at[rows(q)], dst.at[rows(q)], y_send.at[k], y_recv.at[k], y_next[d])

    def c_copy(j, q):
        return remote(held[2 * j].at[rows(q)], held[2 * j + 1].at[rows(q)], c_send.at[4 * j + q], c_recv.at[4 * j + q], sibling)

    def z_copy(d, i, back=0):
        step, q = z_order[d][i]
        k = (0 if d == 1 else len(z_order[1])) + i
        at = slab.at[pl.ds(pl.multiple_of(beside(z, n, -d * (step + back)) * depth + q * part, part), part)]
        return remote(at, at, z_send.at[k], z_recv.at[k], z_next[d])

    def lanes(j, c):
        side = core if c == 0 else 1 - core
        return pl.ds(pl.multiple_of(beside(y, n, j) * 2 * BS + side * BS, BS), BS)

    def unpack(j, c, places):
        ref, where = held[2 * j + c], lanes(j, c)
        slots = range(min(NNZ, places[-1] + 1))
        one_of = {}
        for p in places:
            line = ref[pl.ds(0, TAB), :][p : p + 1, :].astype(jnp.float32)
            for s in slots:
                if p - (RB - NNZ) <= s <= p:
                    one_of[p, s] = (line == float(s)).astype(jnp.bfloat16)

        @pl.loop(0, BS // 16)
        def _(i):
            values = [ref[pl.ds(pl.multiple_of(TAB + s * BS + i * 16, 16), 16), :] for s in slots]
            for p in places:
                terms = [values[s] * one_of[p, s] for s in slots if (p, s) in one_of]
                dense[pl.ds(pl.multiple_of(p * BS + i * 16, 16), 16), where] = functools.reduce(jnp.add, terms)

    def multiply(unit):
        return jnp.dot(dense[pl.ds(unit * 2 * BS, 2 * BS), :], slab[...], preferred_element_type=jnp.float32)

    def spans(rows=2 * BS):
        return [(g, slice(g * GROUP, (g + 1) * GROUP)) for g in range(rows // GROUP)]

    def encode(u, total):
        for g, span in spans():
            values = total[span]
            largest = jnp.maximum(jnp.max(jnp.abs(values), axis=0, keepdims=True), 4e-34)
            send_s[u, g : g + 1, :] = largest * (1.0 / TOP)
            send_x[u, span, :] = jnp.round(values * (TOP / largest)).astype(jnp.int32).astype(jnp.int16)

    def decode(u, g, span):
        return got_x[u, span, :].astype(jnp.int32).astype(jnp.float32) * got_s[u, g : g + 1, :]

    def x_copies(u):
        device = x_next[1 if u % 2 == 0 else -1]
        return (
            remote(send_s.at[u], got_s.at[u], s_send.at[u], s_recv.at[u], device),
            remote(send_x.at[u], got_x.at[u], x_send.at[u], x_recv.at[u], device),
        )

    def x_begin(u, total):
        encode(u, total)
        for copy in x_copies(u):
            begin(copy)

    def x_wait(u):
        for copy in x_copies(u):
            copy.wait_recv()

    def follow(copy_of, after, event):
        for i, at in enumerate(after):
            if at == event:
                for d in (1, -1):
                    begin(copy_of(d, i))

    first, rest = [(d, i) for i, at in enumerate(y_after) if at == -1 for d in (1, -1)], (2, 3)
    for d, i in first[:4] if n > 2 else ():
        begin(y_copy(d, i))
    follow(z_copy, z_after, -1)
    for q in rest:
        pack(q)
    for d, i in first[4:] if n > 2 else first:
        begin(y_copy(d, i))
    for q in range(4):
        begin(c_copy(0, q))

    arrived, passed = {0: {0, 1, 2, 3}}, {0: {0, 1, 2, 3}}
    early, late = list(range(RB // NL)), list(range(RB // NL, RB))
    done = set()
    waited = set()

    def take(j, c, wanted, which):
        if (j, c, which) in done:
            return
        if c == 1:
            for q in wanted:
                if (j, q) not in waited:
                    waited.add((j, q))
                    c_copy(j, q).wait_recv()
        done.add((j, c, which))
        unpack(j, c, early if which == 0 else late)

    def drain(c, source_of):
        for j in range(n):
            have = source_of.get(j, set())
            if {0, 1} <= have:
                take(j, c, (0, 1), 0)
            if {0, 1, 2, 3} <= have:
                take(j, c, (0, 1, 2, 3), 1)

    events = [(Y_STEP * (i + 1), 0, i) for i in range(len(y_order[1]))] + [(Z_STEP * (i + 1), 1, i) for i in range(len(z_order[1]))]
    computed = [0]

    def early_unit(u):
        x_begin(u, multiply(u))

    z_left = len(z_order[1])
    for _, kind, i in sorted(events):
        if kind == 1:
            for d in (1, -1):
                z_copy(d, i, 1).wait_recv()
            follow(z_copy, z_after, i)
            z_left -= 1
            continue
        before = {j: set(v) for j, v in passed.items()}
        for d in (1, -1):
            step, q = y_order[d][i]
            j = (-d * (step + 1)) % n
            y_copy(d, i).wait_recv()
            begin(c_copy(j, q))
            arrived.setdefault(j, set()).add(q)
            passed.setdefault(j, set()).add(q)
        follow(y_copy, y_after, i)
        if i < len(y_order[1]) - 1:
            drain(0, arrived)
            drain(1, before)
            ready = all((j, c, 0) in done for j in range(n) for c in range(2))
            if z_left == 0 and ready and computed[0] < 2:
                early_unit(computed[0])
                computed[0] += 1
    drain(0, arrived)
    drain(1, passed)
    for u in range(computed[0], 2):
        early_unit(u)
    for u in (2, 3):
        early_unit(u)
    for u in (4, 5):
        total = multiply(u)
        x_wait(u - 4)
        x_begin(u, jnp.concatenate([total[span] + decode(u - 4, g, span) for g, span in spans()], axis=0))
    for i in range(2):
        own[i] = multiply(6 + i)
    for i, u in ((0, 3), (1, 2)):
        x_wait(u)
        for g, span in spans():
            own[i, span, :] += decode(u, g, span)
    for i, u in ((0, 4), (1, 5)):
        x_wait(u)
        for g, span in spans():
            total = own[i, span, :] + decode(u, g, span)
            for c in range(total.shape[1] // BS):
                kept = keep[2 * i + g * GROUP // BS, c].astype(jnp.float32)
                at = slice(c * BS, (c + 1) * BS)
                out[pl.ds(2 * i * BS + g * GROUP, GROUP), at] = (total[:, at] * kept).astype(jnp.bfloat16)
    for copy in started:
        copy.wait_send()


def per_device(n, panel_values, slab_values, pattern_panel, pattern_result):
    block = panel_values.shape[1]
    width = slab_values.shape[1]
    depth = slab_values.shape[0]
    sent_y, sent_z = len(panel_order(n, True)), len(ring_order(n, True, 2))
    dma = pltpu.SemaphoreType.DMA
    held = [pltpu.VMEM((TAB + NNZ * BS, BS), jnp.bfloat16) for _ in range(2 * n)]
    half = 2 * BS
    return pl.pallas_call(
        functools.partial(kernel, n),
        out_shape=jax.ShapeDtypeStruct((4 * BS, width), jnp.bfloat16),
        in_specs=[pl.BlockSpec(memory_space=pl.ANY)] * 4,
        out_specs=pl.BlockSpec(memory_space=pltpu.VMEM),
        scratch_shapes=held
        + [
            pltpu.SMEM((RB,), jnp.int32),
            pltpu.SMEM(pattern_result.shape, jnp.int32),
            pltpu.VMEM((RB, BS, BS), jnp.bfloat16),
            pltpu.VMEM((n * depth, width), jnp.bfloat16),
            pltpu.VMEM((RB * BS, n * 2 * BS), jnp.bfloat16),
            pltpu.VMEM((2, half, width), jnp.float32),
            pltpu.VMEM((6, half, width), jnp.int16),
            pltpu.VMEM((6, half // GROUP, width), jnp.float32),
            pltpu.VMEM((6, half, width), jnp.int16),
            pltpu.VMEM((6, half // GROUP, width), jnp.float32),
            dma((4,)),
            dma((2 * sent_y,)),
            dma((2 * sent_y,)),
            dma((4 * n,)),
            dma((4 * n,)),
            dma((2 * sent_z,)),
            dma((2 * sent_z,)),
            dma((6,)),
            dma((6,)),
            dma((6,)),
            dma((6,)),
        ],
        compiler_params=pltpu.CompilerParams(collective_id=0, has_side_effects=True, vmem_limit_bytes=60 * 1024 * 1024),
        cost_estimate=pl.CostEstimate(flops=2 * RB * BS * n * 2 * BS * width, bytes_accessed=1 << 22, transcendentals=0),
    )(panel_values.reshape(RB, BS, block), slab_values, pattern_panel[:, 0], pattern_result)


def solution(mesh):
    placed = (
        P("row", ("layer", "col")),
        P(("layer", "row"), "col"),
        P("row", ("layer", "col")),
        P(("row", "layer"), "col"),
    )
    return jax.shard_map(
        functools.partial(per_device, mesh.shape["row"]),
        mesh=mesh,
        in_specs=placed,
        out_specs=P(("row", "layer"), "col"),
        check_vma=False,
    )
```

```python
import functools

import jax
import jax.numpy as jnp
from jax import lax
from jax.experimental import pallas as pl
from jax.experimental.pallas import tpu as pltpu
from jax.sharding import PartitionSpec as P

BS = 128
RB = 16
NNZ = 8
TAB = 16
NL = 4
UNITS = [((to, 0, r), (to, 1, r)) if to in (0, 2) else ((1, 1 - e, r), (3, e, r)) for to, e in ((2, 0), (1, 0), (1, 1), (0, 0)) for r in (0, 1)]
GROUP = 32
TOP = 32767.0
PIECES = ((0, 2), (2, 2), (4, 2), (6, 2))
SLOT_US, HOP_US, Z_US, Z_LATE = 0.76, 2.7, 2.37, 2.0
WINDOW = 8


def ring_order(n, forward, pieces):
    own = list(range(pieces)) if forward else list(range(pieces))[::-1]
    return [(step, q) for step in range(n // 2) for q in (own if step < n // 2 - 1 else own[: pieces // 2])]


def panel_order(n, forward):
    a, b, c, d = range(len(PIECES)) if forward else (1, 0, 3, 2)
    plan = [(0, a), (0, b), (0, c), (1, a), (1, b), (0, d), (2, a), (2, b), (1, c), (1, d), (3, a), (2, c), (2, d), (3, c)]
    last = n // 2 - 1
    order, ready, now = [], {}, 0.0
    for step, q in plan:
        if step < last or step == last and q in (a, c):
            now = max(now, ready.get(q, 0.0)) + PIECES[q][1] * SLOT_US
            ready[q] = now + HOP_US
            order.append(((step, q), ready[q]))
    return order


def triggers(order, depth, size):
    after = []
    for m, (step, q) in enumerate(order):
        needs = order.index((step - 1, q)) if step else -1
        room = next(e for e in range(-1, m) if sum(size(r) for _, r in order[e + 1 : m + 1]) <= depth)
        after.append(max(after[-1] if after else -1, needs, room))
    return after


def kernel(n, panel_hbm, slab_hbm, flags_hbm, keep_hbm, out, *scratch):
    held = scratch[: 2 * n]
    (flags, keep, panel, slab, dense, own, send_x, send_s, got_x, got_s, own_sem, y_send, y_recv, c_send, c_recv, z_send, z_recv, x_send, x_recv, s_send, s_recv) = scratch[2 * n :]
    col, z, layer = lax.axis_index("col"), lax.axis_index("row"), lax.axis_index("layer")
    y, core = col // 2, lax.rem(col, 2)
    depth = slab_hbm.shape[0]
    part = depth // 2

    def beside(place, count, step):
        return lax.rem(place + step + count, count)

    y_next = {+1: {"col": beside(y, n, 1) * 2 + core}, -1: {"col": beside(y, n, -1) * 2 + core}}
    z_next = {+1: {"row": beside(z, n, 1)}, -1: {"row": beside(z, n, -1)}}
    x_next = {+1: {"layer": beside(layer, NL, 1)}, -1: {"layer": beside(layer, NL, -1)}}
    sibling = {"col": y * 2 + 1 - core}
    neighbours = [y_next[1], y_next[-1], z_next[1], z_next[-1], x_next[1], x_next[-1], sibling]
    barrier = pltpu.get_barrier_semaphore()
    for device in neighbours:
        pl.semaphore_signal(barrier, inc=1, device_id=device, device_id_type=pl.DeviceIdType.MESH)

    flags_in = pltpu.make_async_copy(flags_hbm, flags, own_sem.at[0])
    flags_in.start()
    panel_in = pltpu.make_async_copy(panel_hbm, panel, own_sem.at[1])
    panel_in.start()
    slab_in = pltpu.make_async_copy(slab_hbm, slab.at[pl.ds(pl.multiple_of(z * depth, depth), depth)], own_sem.at[2])
    slab_in.start()
    keep_in = pltpu.make_async_copy(keep_hbm, keep, own_sem.at[3])
    keep_in.start()

    rows_of = []
    for ahead, half, r in sum(UNITS, ()):
        rows_of.append(lax.rem(layer + ahead, NL) * (RB // NL) + half * 2 + r)
    count = jnp.int32(0)
    source = [jnp.int32(0)] * NNZ
    table = jnp.full((TAB, BS), float(NNZ), jnp.float32)
    place_of = lax.broadcasted_iota(jnp.int32, (TAB, BS), 0)
    flags_in.wait()
    for p in range(RB):
        flag = flags[rows_of[p]]
        if p > RB - NNZ:
            count = jnp.maximum(count, p - (RB - NNZ))
        for s in range(max(0, p - (RB - NNZ)), min(p, NNZ - 1) + 1):
            source[s] = jnp.where((flag == 1) & (count == s), rows_of[p], source[s])
        slot = jnp.where(flag == 1, count, NNZ)
        table = jnp.where(place_of == p, slot.astype(jnp.float32), table)
        count = count + flag
    held[0][pl.ds(0, TAB), :] = table.astype(jnp.bfloat16)
    panel_in.wait()

    def pack(q):
        for s in range(PIECES[q][0], sum(PIECES[q])):
            held[0][pl.ds(TAB + s * BS, BS), :] = panel[source[s]]

    pack(0)
    pack(1)
    slab_in.wait()
    keep_in.wait()
    pl.semaphore_wait(barrier, len(neighbours))

    started = []

    def remote(src, dst, send, recv, device):
        return pltpu.make_async_remote_copy(src_ref=src, dst_ref=dst, send_sem=send, recv_sem=recv, device_id=device, device_id_type=pl.DeviceIdType.MESH)

    def begin(copy):
        copy.start()
        started.append(copy)

    def rows(q):
        slot, slots = PIECES[q]
        return pl.ds(0, TAB + slots * BS) if slot == 0 else pl.ds(TAB + slot * BS, slots * BS)

    y_order = {d: [item for item, _ in panel_order(n, d == 1)] for d in (1, -1)}
    z_order = {d: ring_order(n, d == 1, 2) for d in (1, -1)}
    y_after, z_after = triggers(y_order[1], WINDOW, lambda q: PIECES[q][1]), triggers(z_order[1], 2, lambda q: 1)

    def y_copy(d, i):
        step, q = y_order[d][i]
        src, dst = held[2 * ((-d * step) % n)], held[2 * ((-d * (step + 1)) % n)]
        k = (0 if d == 1 else len(y_order[1])) + i
        return remote(src.at[rows(q)], dst.at[rows(q)], y_send.at[k], y_recv.at[k], y_next[d])

    def c_copy(j, q):
        return remote(held[2 * j].at[rows(q)], held[2 * j + 1].at[rows(q)], c_send.at[len(PIECES) * j + q], c_recv.at[len(PIECES) * j + q], sibling)

    def z_copy(d, i, back=0):
        step, q = z_order[d][i]
        k = (0 if d == 1 else len(z_order[1])) + i
        at = slab.at[pl.ds(pl.multiple_of(beside(z, n, -d * (step + back)) * depth + q * part, part), part)]
        return remote(at, at, z_send.at[k], z_recv.at[k], z_next[d])

    def lanes(j, c):
        side = core if c == 0 else 1 - core
        return pl.ds(pl.multiple_of(beside(y, n, j) * 2 * BS + side * BS, BS), BS)

    def unpack(j, c, places):
        ref, where = held[2 * j + c], lanes(j, c)
        slots = range(min(NNZ, places[-1] + 1))
        one_of = {}
        for p in places:
            line = ref[pl.ds(0, TAB), :][p : p + 1, :].astype(jnp.float32)
            for s in slots:
                if p - (RB - NNZ) <= s <= p:
                    one_of[p, s] = (line == float(s)).astype(jnp.bfloat16)

        @pl.loop(0, BS // 16)
        def _(i):
            values = [ref[pl.ds(pl.multiple_of(TAB + s * BS + i * 16, 16), 16), :] for s in slots]
            for p in places:
                terms = [values[s] * one_of[p, s] for s in slots if (p, s) in one_of]
                dense[pl.ds(pl.multiple_of(p * BS + i * 16, 16), 16), where] = functools.reduce(jnp.add, terms)

    def multiply(unit):
        return jnp.dot(dense[pl.ds(unit * 2 * BS, 2 * BS), :], slab[...], preferred_element_type=jnp.float32)

    spans = [(g, slice(g * GROUP, (g + 1) * GROUP)) for g in range(BS // GROUP)]

    def encode(k, total):
        for g, span in spans:
            values = total[span]
            largest = jnp.maximum(jnp.max(jnp.abs(values), axis=0, keepdims=True), 4e-34)
            send_s[k, g : g + 1, :] = largest * (1.0 / TOP)
            send_x[k, span, :] = jnp.round(values * (TOP / largest)).astype(jnp.int32).astype(jnp.int16)

    def decode(k, g, span):
        return got_x[k, span, :].astype(jnp.int32).astype(jnp.float32) * got_s[k, g : g + 1, :]

    def x_copies(k):
        device = x_next[1 if k % 2 == 0 else -1]
        return (
            remote(send_s.at[k], got_s.at[k], s_send.at[k], s_recv.at[k], device),
            remote(send_x.at[k], got_x.at[k], x_send.at[k], x_recv.at[k], device),
        )

    def x_begin(k, total):
        encode(k, total)
        for copy in x_copies(k):
            begin(copy)

    def x_wait(k):
        for copy in x_copies(k):
            copy.wait_recv()

    def follow(copy_of, after, event, sides=(1, -1)):
        for i, at in enumerate(after):
            if at == event:
                for d in sides:
                    begin(copy_of(d, i))

    first = [(d, i) for i, at in enumerate(y_after) if at == -1 for d in (1, -1)]
    packed = {0, 1}
    for d, i in first:
        if y_order[d][i][1] in packed:
            begin(y_copy(d, i))
    follow(z_copy, z_after, -1)
    for q in range(2, len(PIECES)):
        pack(q)
    for d, i in first:
        if y_order[d][i][1] not in packed:
            begin(y_copy(d, i))
    everything = set(range(len(PIECES)))
    for q in range(len(PIECES)):
        begin(c_copy(0, q))

    arrived, passed = {0: set(everything)}, {0: set(everything)}
    tiers = (((0, 1), range(4)), ((0, 1, 2), range(4, 6)), (range(len(PIECES)), range(6, RB)))
    done = set()
    waited = set()

    def drain(c, source_of):
        for j in range(n):
            for tier, (pieces, places) in enumerate(tiers):
                if (j, c, tier) in done or not set(pieces) <= source_of.get(j, set()):
                    continue
                for q in pieces if c == 1 else ():
                    if (j, q) not in waited:
                        waited.add((j, q))
                        c_copy(j, q).wait_recv()
                done.add((j, c, tier))
                unpack(j, c, places)

    events = [(us, 0, i) for i, (_, us) in enumerate(panel_order(n, True))]
    events += [(Z_US * (i + 1) + HOP_US + Z_LATE, 1, i) for i in range(len(z_order[1]))]
    computed = [0]

    def early_unit(u):
        total = multiply(u)
        for side in range(2):
            x_begin(2 * u + side, total[side * BS : (side + 1) * BS])

    z_left = len(z_order[1])
    for _, kind, i in sorted(events):
        if kind == 1:
            for d in (1, -1):
                z_copy(d, i, 1).wait_recv()
                follow(z_copy, z_after, i, (d,))
            z_left -= 1
            continue
        landed = []
        before = {j: set(v) for j, v in passed.items()}
        for d in (1, -1):
            step, q = y_order[d][i]
            j = (-d * (step + 1)) % n
            y_copy(d, i).wait_recv()
            follow(y_copy, y_after, i, (d,))
            landed.append((j, q))
            arrived.setdefault(j, set()).add(q)
            passed.setdefault(j, set()).add(q)
        for j, q in landed:
            begin(c_copy(j, q))
        for turn in range(2):
            u = computed[0]
            if turn == 0 and i >= max(y_after) or turn == 1 and i < max(y_after):
                if z_left == 0 and u < 2 and all((j, c, 0) in done for j in range(n) for c in range(2)):
                    early_unit(u)
                    computed[0] += 1
            if turn == 0 and i < len(y_order[1]) - 1:
                drain(0, arrived)
                drain(1, before)
    drain(0, arrived)
    drain(1, passed)
    for u in range(computed[0], 4):
        early_unit(u)
    for u in (4, 5):
        total = multiply(u)
        for side in range(2):
            k = 2 * (u - 4) + side
            x_wait(k)
            x_begin(2 * u + side, jnp.concatenate([total[side * BS :][span] + decode(k, g, span) for g, span in spans], axis=0))
    for r in range(2):
        total = multiply(6 + r)
        for half in range(2):
            own[half * 2 + r] = total[half * BS : (half + 1) * BS]
    for r in range(2):
        for half in range(2):
            k = 2 * (2 + r) + 1 - half
            x_wait(k)
            for g, span in spans:
                own[half * 2 + r, span, :] += decode(k, g, span)
    for r in range(2):
        for half in range(2):
            k = 2 * (4 + r) + half
            x_wait(k)
            for g, span in spans:
                total = own[half * 2 + r, span, :] + decode(k, g, span)
                for c in range(total.shape[1] // BS):
                    kept = keep[half * 2 + r, c].astype(jnp.float32)
                    at = slice(c * BS, (c + 1) * BS)
                    out[pl.ds((half * 2 + r) * BS + g * GROUP, GROUP), at] = (total[:, at] * kept).astype(jnp.bfloat16)
    for copy in started:
        copy.wait_send()


def per_device(n, panel_values, slab_values, pattern_panel, pattern_result):
    block = panel_values.shape[1]
    width = slab_values.shape[1]
    depth = slab_values.shape[0]
    sent_y, sent_z = len(panel_order(n, True)), len(ring_order(n, True, 2))
    dma = pltpu.SemaphoreType.DMA
    held = [pltpu.VMEM((TAB + NNZ * BS, BS), jnp.bfloat16) for _ in range(2 * n)]
    return pl.pallas_call(
        functools.partial(kernel, n),
        out_shape=jax.ShapeDtypeStruct((4 * BS, width), jnp.bfloat16),
        in_specs=[pl.BlockSpec(memory_space=pl.ANY)] * 4,
        out_specs=pl.BlockSpec(memory_space=pltpu.VMEM),
        scratch_shapes=held
        + [
            pltpu.SMEM((RB,), jnp.int32),
            pltpu.SMEM(pattern_result.shape, jnp.int32),
            pltpu.VMEM((RB, BS, BS), jnp.bfloat16),
            pltpu.VMEM((n * depth, width), jnp.bfloat16),
            pltpu.VMEM((RB * BS, n * 2 * BS), jnp.bfloat16),
            pltpu.VMEM((4, BS, width), jnp.float32),
            pltpu.VMEM((12, BS, width), jnp.int16),
            pltpu.VMEM((12, BS // GROUP, width), jnp.float32),
            pltpu.VMEM((12, BS, width), jnp.int16),
            pltpu.VMEM((12, BS // GROUP, width), jnp.float32),
            dma((4,)),
            dma((2 * sent_y,)),
            dma((2 * sent_y,)),
            dma((len(PIECES) * n,)),
            dma((len(PIECES) * n,)),
            dma((2 * sent_z,)),
            dma((2 * sent_z,)),
            dma((12,)),
            dma((12,)),
            dma((12,)),
            dma((12,)),
        ],
        compiler_params=pltpu.CompilerParams(collective_id=0, has_side_effects=True, vmem_limit_bytes=60 * 1024 * 1024),
        cost_estimate=pl.CostEstimate(flops=2 * RB * BS * n * 2 * BS * width, bytes_accessed=1 << 22, transcendentals=0),
    )(panel_values.reshape(RB, BS, block), slab_values, pattern_panel[:, 0], pattern_result)


def solution(mesh):
    placed = (
        P("row", ("layer", "col")),
        P(("layer", "row"), "col"),
        P("row", ("layer", "col")),
        P(("row", "layer"), "col"),
    )
    return jax.shard_map(
        functools.partial(per_device, mesh.shape["row"]),
        mesh=mesh,
        in_specs=placed,
        out_specs=P(("row", "layer"), "col"),
        check_vma=False,
    )
```
